32 devices in a mesh: grp: 2 (over x), lat: 16 (over z, y, core).
Axes of the slice: x: 2, y: 2, z: 4, core: 2. Of those that a mesh axis runs over, the one named last changes fastest.
Arguments:
- state_field: bfloat16 [8, 48, 180, 768], P('grp', 'lat'), parts along dimension 0, may hold values from -6 to 6
- norm1_gain: float32 [768], replicated, may hold values from 0.25 to 1.75
- norm1_shift: float32 [768], replicated, may hold values from -3 to 3
- spec_w1: bfloat16 [2, 8, 96, 96], replicated, may hold values from -0.4375 to 0.4375
- spec_b1: float32 [2, 768], replicated, may hold values from -3 to 3
- spec_w2: bfloat16 [2, 8, 96, 96], replicated, may hold values from -0.625 to 0.625
- spec_b2: float32 [2, 768], replicated, may hold values from -3 to 3
- norm2_gain: float32 [768], replicated, may hold values from 0.25 to 1.75
- norm2_shift: float32 [768], replicated, may hold values from -3 to 3
- fc1_weight: bfloat16 [768, 3072], replicated, may hold values from -0.21875 to 0.21875
- fc1_bias: float32 [3072], replicated, may hold values from -3 to 3
- fc2_weight: bfloat16 [3072, 768], replicated, may hold values from -0.109375 to 0.109375
- fc2_bias: float32 [768], replicated, may hold values from -3 to 3
Outputs:
- block_out: bfloat16 [8, 48, 180, 768], P('grp', 'lat'), parts along dimension 0
The draws below stay inside these ranges and needn't reach their ends.
There are 2 independent parts, one for each index of `grp`. The reference program is written for one: setup_inputs(seed, part) draws one part's arguments, and reference() takes and returns one part's arrays. A program takes and returns all parts, laid end to end along the dimension named above; an argument that names none is the same for every part. Nothing has to cross between parts.
All inputs are finite; a program needn't handle non-finite values.
Results may differ from the reference program's by a relative error of at most 0.007.
Values may be sent and summed in bfloat16 or wider, within the bound.
No kernel may reach another device: no remote copies, remote signals or barrier semaphores. Data moves between devices by JAX's collectives and lax.ppermute only.
A program may use at most 128 MiB of HBM per device.

```python
import math
import jax
import jax.numpy as jnp
from jax import lax

D = 768
NB = 8
FF = 3072
W = 180
KW = 64
SAMPLES = 4
BS = 96
H = 48


def steps_of(own_key, shape, shards, least, largest):
    def one(position, parts):
        draws = jax.random.uniform(jax.random.fold_in(jax.random.fold_in(own_key, 6), position), (parts,), jnp.float32, least / len(shards), largest / len(shards))
        return jnp.repeat(jnp.exp(draws), shape[position] // parts).reshape((-1,) + (1,) * (len(shape) - position - 1))

    factor_of = one(*shards[0])
    for cut in shards[1:]:
        factor_of = factor_of * one(*cut)
    return factor_of


def gaussian(own_key, shape, deviation, bound, pieces=(), kind=jnp.bfloat16):
    values = jax.random.normal(own_key, shape, jnp.float32) * deviation
    if len(pieces) > 0:
        values = steps_of(own_key, shape, pieces, -0.22, 0.18) * values
    return jnp.clip(values, min=-bound, max=bound).astype(kind)


def setup_inputs(seed: int = 0, part: int = 0) -> dict:
    keys = jax.random.split(jax.random.key(seed), 14)
    own_keys = jax.random.split(jax.random.fold_in(keys[13], part), 14)
    state_field = gaussian(own_keys[0], (SAMPLES, H, W, D), 1.0, 6.0, ((1, 16),))
    norm1_gain = jnp.clip(1.0 + 0.15 * jax.random.normal(keys[1], (D,), jnp.float32), 0.25, 1.75)
    norm1_shift = gaussian(keys[2], (D,), 0.4, 3.0, (), jnp.float32)
    spec_w1 = gaussian(keys[3], (2, NB, BS, BS), (2 * BS) ** -0.5, 0.4375)
    spec_b1 = gaussian(keys[4], (2, D), 0.4, 3.0, (), jnp.float32)
    spec_w2 = gaussian(keys[5], (2, NB, BS, BS), BS ** -0.5, 0.625)
    spec_b2 = gaussian(keys[6], (2, D), 0.3, 3.0, (), jnp.float32)
    norm2_gain = jnp.clip(1.0 + 0.15 * jax.random.normal(keys[7], (D,), jnp.float32), 0.25, 1.75)
    norm2_shift = gaussian(keys[8], (D,), 0.4, 3.0, (), jnp.float32)
    fc1_weight = gaussian(keys[9], (D, FF), D ** -0.5, 0.21875)
    fc1_bias = gaussian(keys[10], (FF,), 0.5, 3.0, (), jnp.float32)
    fc2_weight = gaussian(keys[11], (FF, D), FF ** -0.5, 0.109375)
    fc2_bias = gaussian(keys[12], (D,), 0.4, 3.0, (), jnp.float32)
    return dict(state_field=state_field, norm1_gain=norm1_gain, norm1_shift=norm1_shift, spec_w1=spec_w1, spec_b1=spec_b1, spec_w2=spec_w2, spec_b2=spec_b2, norm2_gain=norm2_gain, norm2_shift=norm2_shift, fc1_weight=fc1_weight, fc1_bias=fc1_bias, fc2_weight=fc2_weight, fc2_bias=fc2_bias)


def lon_tables(width, kept):
    along = jnp.arange(width, dtype=jnp.int32)
    waves = jnp.arange(kept, dtype=jnp.int32)
    phase = along[:, None] * waves[None, :] % width
    angle = 2.0 * math.pi / width * phase.astype(jnp.float32)
    factor = 1.0 / math.sqrt(width)
    forward = jnp.concatenate([jnp.cos(angle), -jnp.sin(angle)], axis=1) * factor
    weight_k = jnp.where(waves == 0, 1.0, 2.0).astype(jnp.float32)
    inverse = jnp.concatenate([jnp.cos(angle) * weight_k, -jnp.sin(angle) * weight_k], axis=1).T * factor
    return (forward.astype(jnp.bfloat16), inverse.astype(jnp.bfloat16))

def lat_tables(length):
    index = jnp.arange(length, dtype=jnp.int32)
    phase = index[:, None] * index[None, :] % length
    angle = 2.0 * math.pi / length * phase.astype(jnp.float32)
    factor = 1.0 / math.sqrt(length)
    return ((jnp.cos(angle) * factor).astype(jnp.bfloat16), (jnp.sin(angle) * factor).astype(jnp.bfloat16))

def layer_norm(values, gain, shift):
    center = lax.optimization_barrier(jnp.mean(values, axis=-1, keepdims=True))
    spread = lax.optimization_barrier(jnp.mean(jnp.square(values - center), axis=-1, keepdims=True))
    return (values - center) * lax.rsqrt(spread + 1e-05) * gain + shift

def matmul(left, right):
    return jnp.dot(left, right, preferred_element_type=jnp.float32)

def block_product(left, weight):
    return jnp.einsum('rnb,nbe->rne', left.astype(jnp.float32), weight.astype(jnp.float32))

def block_mix(part_re, part_im, weight, bias):
    count = part_re.shape[0]
    blocks = weight.shape[1]
    inner = weight.shape[2]
    left_re = part_re.reshape(count, blocks, inner)
    left_im = part_im.reshape(count, blocks, inner)
    out_re = block_product(left_re, weight[0]) - block_product(left_im, weight[1])
    out_im = block_product(left_re, weight[1]) + block_product(left_im, weight[0])
    return (out_re.reshape(count, -1) + bias[0], out_im.reshape(count, -1) + bias[1])

def reference(state_field, norm1_gain, norm1_shift, spec_w1, spec_b1, spec_w2, spec_b2, norm2_gain, norm2_shift, fc1_weight, fc1_bias, fc2_weight, fc2_bias):
    forward, inverse = lon_tables(W, KW)
    lat_cos, lat_sin = lat_tables(H)

    def one_sample(field):
        values = field.astype(jnp.float32)
        normed = layer_norm(values, norm1_gain, norm1_shift).astype(jnp.bfloat16)
        spectrum = jnp.einsum('hwc,wk->hkc', normed.astype(jnp.float32), forward.astype(jnp.float32)).astype(jnp.bfloat16)
        a_re = spectrum[:, :KW].reshape(H, KW * D)
        a_im = spectrum[:, KW:].reshape(H, KW * D)
        b_re = (matmul(lat_cos, a_re) + matmul(lat_sin, a_im)).astype(jnp.bfloat16)
        b_im = (matmul(lat_cos, a_im) - matmul(lat_sin, a_re)).astype(jnp.bfloat16)
        first_re, first_im = block_mix(b_re.reshape(H * KW, D), b_im.reshape(H * KW, D), spec_w1, spec_b1)
        first_re = jax.nn.relu(first_re).astype(jnp.bfloat16)
        first_im = jax.nn.relu(first_im).astype(jnp.bfloat16)
        second_re, second_im = block_mix(first_re, first_im, spec_w2, spec_b2)
        second_re = (jnp.sign(second_re) * jnp.maximum(jnp.abs(second_re) - 0.01, 0.0)).astype(jnp.bfloat16).reshape(H, KW * D)
        second_im = (jnp.sign(second_im) * jnp.maximum(jnp.abs(second_im) - 0.01, 0.0)).astype(jnp.bfloat16).reshape(H, KW * D)
        y_re = (matmul(lat_cos, second_re) - matmul(lat_sin, second_im)).astype(jnp.bfloat16)
        y_im = (matmul(lat_cos, second_im) + matmul(lat_sin, second_re)).astype(jnp.bfloat16)
        joined = jnp.concatenate([y_re.reshape(H, KW, D), y_im.reshape(H, KW, D)], axis=1)
        filtered = jnp.einsum('hkc,kw->hwc', joined.astype(jnp.float32), inverse.astype(jnp.float32))
        mixed_state = filtered + normed.astype(jnp.float32) + values
        second_norm = layer_norm(mixed_state, norm2_gain, norm2_shift).astype(jnp.bfloat16).reshape(H * W, D)
        hidden = jax.nn.gelu(matmul(second_norm, fc1_weight) + fc1_bias).astype(jnp.bfloat16)
        result = mixed_state.reshape(H * W, D) + matmul(hidden, fc2_weight) + fc2_bias
        return result.astype(jnp.bfloat16).reshape(H, W, D)
    return lax.map(one_sample, state_field)
```

```python
import functools
import math

import jax
import jax.numpy as jnp
import numpy as np
from jax import lax
from jax.experimental import pallas as pl
from jax.experimental.pallas import tpu as pltpu
from jax.sharding import PartitionSpec as P

KW = 64
BF = jnp.bfloat16
F32 = jnp.float32
FIRST_CHUNKS = (2, 2)
SECOND_CHUNKS = (2, 2)


def lon_tables(width, kept, chips):
    along = np.arange(width)
    waves = np.arange(kept)
    angle = 2.0 * math.pi / width * (along[:, None] * waves[None, :] % width)
    factor = 1.0 / math.sqrt(width)
    weight_k = np.where(waves == 0, 1.0, 2.0)
    split = (width, chips, kept // chips)
    forward = np.stack(
        [np.cos(angle).reshape(split), -np.sin(angle).reshape(split)], axis=2
    ).reshape(width, 2 * kept)
    inverse = np.stack(
        [(np.cos(angle) * weight_k).reshape(split), (-np.sin(angle) * weight_k).reshape(split)],
        axis=2,
    ).reshape(width, 2 * kept)
    to_bf = lambda t: jnp.asarray((t * factor).astype(np.float32).astype(jnp.bfloat16))
    return to_bf(forward.T), to_bf(inverse)


def lat_tables(length, waves):
    index = np.arange(length)
    angle = 2.0 * math.pi / length * (index[:, None] * index[None, :] % length)
    cos = np.cos(angle) / math.sqrt(length)
    sin = np.sin(angle) / math.sqrt(length)
    eye = np.eye(waves)
    parts = np.array([[cos, sin], [-sin, cos]])
    size = 2 * length * waves
    forward = np.einsum("pqmh,kl->pmkhql", parts, eye).reshape(size, size)
    parts = np.array([[cos, -sin], [sin, cos]])
    inverse = np.einsum("pqhm,kl->hpkqml", parts, eye).reshape(size, size)
    to_bf = lambda t: jnp.asarray(t.astype(np.float32).astype(jnp.bfloat16))
    return to_bf(forward), to_bf(inverse)


def normalize(values, gain, shift):
    center = jnp.mean(values, axis=-1, keepdims=True)
    away = values - center
    spread = jnp.mean(away * away, axis=-1, keepdims=True)
    return away * lax.rsqrt(spread + 1e-05) * gain + shift


def dot(left, right):
    return jnp.dot(left, right, preferred_element_type=F32)


def forward_kernel(place, x_ref, gain, shift, table, own_ref, other_ref, spec):
    chips = own_ref.shape[0]
    half = own_ref.shape[3]
    rows = x_ref.shape[1]
    span = own_ref.shape[2] // rows
    chip = place[0] // 2
    core = place[0] % 2
    for r in range(rows):
        normed = normalize(x_ref[0, r].astype(F32), gain[...], shift[...]).astype(BF)
        spec[r] = dot(table[...], normed)
    near = pl.ds(pl.multiple_of(core * half, 128), half)
    far = pl.ds(pl.multiple_of((1 - core) * half, 128), half)
    for m in range(chips):
        source = pl.ds(pl.multiple_of((chip ^ m) * span, 8), span)
        for r in range(rows):
            own_ref[m, 0, r * span : (r + 1) * span, :] = spec[r, source, near].astype(BF)
            other_ref[m, 0, r * span : (r + 1) * span, :] = spec[r, source, far].astype(BF)


def forward_part(place, state, gain, shift, table, start, count, chips):
    rows, width, chans = state.shape[1:]
    block = rows * (table.shape[0] // chips)
    half = chans // 2
    out = jax.ShapeDtypeStruct((chips, count, block, half), BF)
    out_spec = pl.BlockSpec((chips, 1, block, half), lambda s, p: (0, s, 0, 0))
    whole = lambda s, p: (0, 0)
    return pl.pallas_call(
        forward_kernel,
        grid_spec=pltpu.PrefetchScalarGridSpec(
            num_scalar_prefetch=1,
            grid=(count,),
            in_specs=[
                pl.BlockSpec((1, rows, width, chans), lambda s, p: (s + start, 0, 0, 0)),
                pl.BlockSpec((1, chans), whole),
                pl.BlockSpec((1, chans), whole),
                pl.BlockSpec(table.shape, whole),
            ],
            out_specs=[out_spec, out_spec],
            scratch_shapes=[pltpu.VMEM((rows, table.shape[0], chans), F32)],
        ),
        out_shape=[out, out],
        compiler_params=pltpu.CompilerParams(vmem_limit_bytes=24 * 2**20),
        cost_estimate=pl.CostEstimate(
            flops=2 * count * rows * width * chans * table.shape[0],
            bytes_accessed=2 * count * rows * width * chans * 2,
            transcendentals=0,
        ),
        name="lon_forward",
    )(place, state, gain, shift, table)


def mix_kernel(chips, place, *refs):
    parts = refs[:chips]
    lat_in, w_one, b_one, w_two, b_two, lat_out = refs[chips : chips + 6]
    own_ref, other_ref, gathered, spread = refs[chips + 6 :]
    block = own_ref.shape[2]
    half = own_ref.shape[3]
    size = lat_in.shape[0]
    me = place[0]
    for m in range(chips):
        for e in range(2):
            where = pl.ds(pl.multiple_of((me ^ (2 * m + e)) * block, 8), block)
            gathered[where, :] = parts[m][0, e].astype(gathered.dtype)
    modes = dot(lat_in[...], gathered[...].astype(BF)).astype(BF)
    modes = jnp.concatenate([modes[: size // 2], modes[size // 2 :]], axis=1)
    first = jnp.maximum(dot(modes, w_one[...]) + b_one[...], 0.0).astype(BF)
    second = dot(first, w_two[...]) + b_two[...]
    second = second - jnp.clip(second, -0.01, 0.01)
    second = second.astype(BF)
    second = jnp.concatenate([second[:, :half], second[:, half:]], axis=0)
    spread[...] = dot(lat_out[...], second).astype(spread.dtype)
    for m in range(chips):
        for e, out_ref in enumerate((own_ref, other_ref)):
            where = pl.ds(pl.multiple_of((me ^ (2 * m + e)) * block, 8), block)
            out_ref[m, 0] = spread[where, :].astype(BF)


def mix_part(place, parts, lat_in, w_one, b_one, w_two, b_two, lat_out):
    chips = len(parts)
    count, pair, block, half = parts[0].shape
    size = lat_in.shape[0]
    kind = BF if block % 16 == 0 else F32
    out = jax.ShapeDtypeStruct((chips, count, block, half), BF)
    out_spec = pl.BlockSpec((chips, 1, block, half), lambda s, p: (0, s, 0, 0))
    whole = lambda s, p: (0, 0)
    table = lambda t: pl.BlockSpec(t.shape, whole)
    return pl.pallas_call(
        functools.partial(mix_kernel, chips),
        grid_spec=pltpu.PrefetchScalarGridSpec(
            num_scalar_prefetch=1,
            grid=(count,),
            in_specs=[pl.BlockSpec((1, pair, block, half), lambda s, p: (s, 0, 0, 0))] * chips
            + [table(t) for t in (lat_in, w_one, b_one, w_two, b_two, lat_out)],
            out_specs=[out_spec, out_spec],
            scratch_shapes=[pltpu.VMEM((size, half), kind), pltpu.VMEM((size, half), kind)],
        ),
        out_shape=[out, out],
        compiler_params=pltpu.CompilerParams(vmem_limit_bytes=32 * 2**20),
        cost_estimate=pl.CostEstimate(
            flops=4 * count * (size * size * half + size // 2 * 4 * half * half),
            bytes_accessed=4 * count * size * half * 2,
            transcendentals=0,
        ),
        name="mix_modes",
    )(place, *parts, lat_in, w_one, b_one, w_two, b_two, lat_out)


def final_kernel(chips, place, *refs):
    parts = refs[:chips]
    x_ref, gain1, shift1, table, gain2, shift2, fc1, bias1, fc2, bias2 = refs[chips : chips + 10]
    out_ref, spec, mixed, act, total = refs[-5:]
    rows = x_ref.shape[1]
    width = x_ref.shape[2]
    half = parts[0].shape[3]
    span = parts[0].shape[2] // rows
    pitch = mixed.shape[0] // rows
    chip = place[0] // 2
    core = place[0] % 2
    near = pl.ds(pl.multiple_of(core * half, 128), half)
    far = pl.ds(pl.multiple_of((1 - core) * half, 128), half)
    for m in range(chips):
        where = pl.ds(pl.multiple_of((chip ^ m) * span, 8), span)
        for r in range(rows):
            cut = slice(r * span, (r + 1) * span)
            spec[r, where, near] = parts[m][0, 0, cut, :].astype(spec.dtype)
            spec[r, where, far] = parts[m][0, 1, cut, :].astype(spec.dtype)
    for r in range(rows):
        values = x_ref[0, r].astype(F32)
        normed = normalize(values, gain1[...], shift1[...]).astype(BF).astype(F32)
        state = dot(table[...], spec[r].astype(BF)) + normed + values
        mixed[r * pitch : r * pitch + width, :] = state
        act[r * pitch : r * pitch + width, :] = normalize(state, gain2[...], shift2[...]).astype(BF)
    hidden = fc1.shape[1]
    step = hidden // 4
    normed2 = act[...]
    for f in range(4):
        cut = slice(f * step, (f + 1) * step)
        inner = dot(normed2, fc1[:, cut]) + bias1[:, cut]
        inner = jax.nn.gelu(inner).astype(BF)
        piece = dot(inner, fc2[cut, :])
        if f == 0:
            total[...] = piece
        else:
            total[...] += piece
    for r in range(rows):
        cut = slice(r * pitch, r * pitch + width)
        out_ref[0, r] = (mixed[cut, :] + total[cut, :] + bias2[...]).astype(BF)


def final_part(place, parts, state, vectors1, table, vectors2, fc1, bias1, fc2, bias2, start, so_far):
    chips = len(parts)
    count, pair, block, half = parts[0].shape
    rows, width, chans = state.shape[1:]
    span = block // rows
    pitch = (width + 15) // 16 * 16
    kind = BF if span % 16 == 0 else F32
    whole = lambda s, p: (0, 0)
    table_spec = lambda t: pl.BlockSpec(t.shape, whole)
    token_spec = pl.BlockSpec((1, rows, width, chans), lambda s, p: (s + start, 0, 0, 0))
    operands = [state, *vectors1, table, *vectors2, fc1, bias1, fc2, bias2]
    in_specs = [pl.BlockSpec((1, pair, block, half), lambda s, p: (s, 0, 0, 0))] * chips
    in_specs += [token_spec] + [table_spec(t) for t in operands[1:]]
    aliases = {}
    if so_far is not None:
        aliases = {1 + len(in_specs): 0}
        in_specs += [pl.BlockSpec(memory_space=pl.ANY)]
        operands.append(so_far)
    return pl.pallas_call(
        functools.partial(final_kernel, chips),
        grid_spec=pltpu.PrefetchScalarGridSpec(
            num_scalar_prefetch=1,
            grid=(count,),
            in_specs=in_specs,
            out_specs=token_spec,
            scratch_shapes=[
                pltpu.VMEM((rows, chips * span, chans), kind),
                pltpu.VMEM((rows * pitch, chans), F32),
                pltpu.VMEM((rows * pitch, chans), BF),
                pltpu.VMEM((rows * pitch, chans), F32),
            ],
        ),
        out_shape=jax.ShapeDtypeStruct(state.shape, BF),
        input_output_aliases=aliases,
        compiler_params=pltpu.CompilerParams(vmem_limit_bytes=48 * 2**20),
        cost_estimate=pl.CostEstimate(
            flops=4 * count * rows * width * chans * fc1.shape[1],
            bytes_accessed=4 * count * rows * width * chans + 4 * chans * fc1.shape[1],
            transcendentals=count * rows * width * fc1.shape[1],
        ),
        name="channel_mlp",
    )(place, *parts, *operands)


def mixing_weights(weight, bias, core):
    blocks = weight.shape[1] // 2
    inner = weight.shape[2]
    half = blocks * inner
    own = lax.dynamic_slice_in_dim(weight, core * blocks, blocks, 1)
    eye = jnp.eye(blocks, dtype=weight.dtype)
    wide = (own[:, :, :, None, :] * eye[None, :, None, :, None]).reshape(2, half, half)
    matrix = jnp.concatenate(
        [
            jnp.concatenate([wide[0], wide[1]], axis=1),
            jnp.concatenate([-wide[1], wide[0]], axis=1),
        ],
        axis=0,
    )
    return matrix, lax.dynamic_slice_in_dim(bias, core * half, half, 1).reshape(1, 2 * half)


def swap_cores(array, devices):
    return lax.ppermute(array, "lat", [(i, i ^ 1) for i in range(devices)])


def swap_chips(own, other, devices):
    parts = []
    for m in range(own.shape[0]):
        part = jnp.stack([own[m], other[m]], axis=1)
        if m > 0:
            part = lax.ppermute(part, "lat", [(i, i ^ (2 * m)) for i in range(devices)])
        parts.append(part)
    return parts


def local(devices, *args):
    (state, gain1, shift1, w_one, b_one, w_two, b_two, gain2, shift2, fc1, bias1, fc2, bias2) = args
    samples, rows, width, chans = state.shape
    chips = devices // 2
    me = lax.axis_index("lat")
    place = me.astype(jnp.int32).reshape(1)
    core = me % 2
    row = lambda v: v.reshape(1, -1)
    forward, inverse = lon_tables(width, KW, chips)
    lat_in, lat_out = lat_tables(rows * devices, KW // chips)
    mix_one = mixing_weights(w_one, b_one, core)
    mix_two = mixing_weights(w_two, b_two, core)

    middle = []
    start = 0
    for count in FIRST_CHUNKS:
        own, other = forward_part(
            place, state, row(gain1), row(shift1), forward, start, count, chips
        )
        parts = swap_chips(own, swap_cores(other, devices), devices)
        middle.append(mix_part(place, parts, lat_in, *mix_one, *mix_two, lat_out))
        start += count

    result = None
    start = 0
    for (own, other), count in zip(middle, SECOND_CHUNKS):
        parts = swap_chips(own, swap_cores(other, devices), devices)
        result = final_part(
            place,
            parts,
            state,
            (row(gain1), row(shift1)),
            inverse,
            (row(gain2), row(shift2)),
            fc1,
            row(bias1),
            fc2,
            row(bias2),
            start,
            result,
        )
        start += count
    return result


def solution(mesh):
    tokens = P("grp", "lat", None, None)
    return jax.shard_map(
        functools.partial(local, mesh.shape["lat"]),
        mesh=mesh,
        in_specs=(tokens,) + (P(),) * 12,
        out_specs=tokens,
        check_vma=False,
    )
```

```python
import functools
import math

import jax
import jax.numpy as jnp
import numpy as np
from jax import lax
from jax.experimental import pallas as pl
from jax.experimental.pallas import tpu as pltpu
from jax.sharding import PartitionSpec as P

KW = 64
BF = jnp.bfloat16
F32 = jnp.float32
SMALL = pl.CostEstimate(flops=1, bytes_accessed=1, transcendentals=0)
FIRST = (2, 2)
SECOND = (1, 1, 1)


def lon_tables(width, kept, chips):
    along = np.arange(width)
    waves = np.arange(kept)
    angle = 2.0 * math.pi / width * (along[:, None] * waves[None, :] % width)
    factor = 1.0 / math.sqrt(width)
    weight_k = np.where(waves == 0, 1.0, 2.0)
    split = (width, chips, kept // chips)
    forward = np.stack(
        [np.cos(angle).reshape(split), -np.sin(angle).reshape(split)], axis=2
    ).reshape(width, 2 * kept)
    inverse = np.stack(
        [(np.cos(angle) * weight_k).reshape(split), (-np.sin(angle) * weight_k).reshape(split)],
        axis=2,
    ).reshape(width, 2 * kept)
    return ((forward * factor).astype(np.float32).T, (inverse * factor).astype(np.float32))


def lat_tables(length, waves):
    index = np.arange(length)
    angle = 2.0 * math.pi / length * (index[:, None] * index[None, :] % length)
    cos = np.cos(angle) / math.sqrt(length)
    sin = np.sin(angle) / math.sqrt(length)
    eye = np.eye(waves)
    parts = np.array([[cos, sin], [-sin, cos]])
    size = 2 * length * waves
    forward = np.einsum("pqmh,kl->pmkhql", parts, eye).reshape(size, size)
    parts = np.array([[cos, -sin], [sin, cos]])
    inverse = np.einsum("pqhm,kl->hpkqml", parts, eye).reshape(size, size)
    to_bf = lambda t: jnp.asarray(t.astype(np.float32).astype(jnp.bfloat16))
    return to_bf(forward), to_bf(inverse)


def over_samples(table, first, count, samples):
    pick = np.eye(samples, dtype=table.dtype)[first : first + count]
    waves, width = table.shape
    wide = pick[:, None, None, :] * table[None, :, :, None]
    return jnp.asarray(wide.reshape(count * waves, width * samples).astype(jnp.bfloat16))


def normalize(values, gain, shift):
    center = jnp.mean(values, axis=-1, keepdims=True)
    away = values - center
    spread = jnp.mean(away * away, axis=-1, keepdims=True)
    return away * lax.rsqrt(spread + 1e-05) * gain[None, :] + shift[None, :]


def dot(left, right):
    return jnp.dot(left, right, preferred_element_type=F32)


def forward_kernel(place, x_hbm, gain_hbm, shift_hbm, table_hbm, *refs):
    outs = refs[:-7]
    x, flat, gain, shift, table, spec, sems = refs[-7:]
    chips, rows, _, span, half = outs[0].shape
    width, samples, chans = x_hbm.shape[1:]
    copies = [
        pltpu.make_async_copy(x_hbm.at[r], x.at[r], sems.at[r]) for r in range(rows)
    ] + [
        pltpu.make_async_copy(source, target, sems.at[rows + i])
        for i, (source, target) in enumerate(
            ((gain_hbm, gain), (shift_hbm, shift), (table_hbm, table))
        )
    ]
    for copy in copies[:1] + copies[rows:] + copies[1:rows]:
        copy.start()
    chip = place[0] // 2
    core = place[0] % 2
    for copy in copies[rows:]:
        copy.wait()
    for r in range(rows):
        copies[r].wait()
        tokens = x[r].astype(F32).reshape(width * samples, chans)
        normed = normalize(tokens, gain[...], shift[...]).astype(BF).astype(F32)
        for tile in range(flat.shape[0]):
            flat[tile] = normed[:, tile * 128 : (tile + 1) * 128]
        start = 0
        for other, *own in (outs[i : i + chips + 1] for i in range(0, len(outs), chips + 1)):
            for s in range(other.shape[2]):
                pick = pl.ds(start + s, width, stride=samples)
                values = jnp.concatenate([flat[t, pick, :] for t in range(flat.shape[0])], axis=1)
                spec[...] = dot(table[...], values.astype(BF))
                for m in range(chips):
                    where = pl.ds(pl.multiple_of((chip ^ m) * span, 8), span)
                    for e in range(2):
                        lanes = pl.ds(pl.multiple_of((core ^ e) * half, 128), half)
                        piece = spec[where, lanes].astype(BF)
                        if e == 0:
                            own[m][r, s] = piece
                        else:
                            other[m, r, s] = piece
            start += other.shape[2]


def forward_part(place, state, gain, shift, table, counts, chips):
    rows, width, samples, chans = state.shape
    waves = table.shape[0]
    outs = []
    for count in counts:
        piece = (rows, count, waves // chips, chans // 2)
        outs += [jax.ShapeDtypeStruct(s, BF) for s in [(chips,) + piece] + [piece] * chips]
    vmem = pl.BlockSpec(memory_space=pltpu.VMEM)
    hbm = pl.BlockSpec(memory_space=pltpu.HBM)
    operands = [state, gain, shift, table]
    out = pl.pallas_call(
        forward_kernel,
        in_specs=[pl.BlockSpec(memory_space=pltpu.SMEM)] + [hbm] * len(operands),
        out_specs=[vmem] * len(outs),
        scratch_shapes=[
            pltpu.VMEM(state.shape, BF),
            pltpu.VMEM((chans // 128, width * samples, 128), F32),
            pltpu.VMEM(gain.shape, F32),
            pltpu.VMEM(shift.shape, F32),
            pltpu.VMEM(table.shape, BF),
            pltpu.VMEM((waves, chans), F32),
            pltpu.SemaphoreType.DMA((rows + 3,)),
        ],
        out_shape=outs,
        compiler_params=pltpu.CompilerParams(vmem_limit_bytes=56 * 2**20),
        cost_estimate=SMALL,
        name="lon_forward",
    )(place, *operands)
    return [out[i : i + chips + 1] for i in range(0, len(out), chips + 1)]


def residual_kernel(x, gain, shift, _, out):
    for r in range(x.shape[0]):
        tokens = x[r].astype(F32).reshape(out.shape[1:])
        out[r] = tokens + normalize(tokens, gain[...], shift[...]).astype(BF).astype(F32)


def residual_part(state, gain, shift, after):
    rows, width, samples, chans = state.shape
    vmem = pl.BlockSpec(memory_space=pltpu.VMEM)
    return pl.pallas_call(
        residual_kernel,
        in_specs=[vmem] * 3 + [pl.BlockSpec(memory_space=pl.ANY)],
        out_specs=vmem,
        out_shape=jax.ShapeDtypeStruct((rows, width * samples, chans), F32),
        compiler_params=pltpu.CompilerParams(vmem_limit_bytes=16 * 2**20),
        cost_estimate=SMALL,
        name="residual",
    )(state, gain, shift, after)


def widen(raw, core, wide):
    blocks, inner = raw.shape[1] // 2, raw.shape[2]
    size = wide.shape[0]
    half = size // 2
    column = lax.broadcasted_iota(jnp.int32, (inner, size), 1)
    row = lax.broadcasted_iota(jnp.int32, (inner, size), 0)
    for n in range(blocks):
        to_re = (column == row + n * inner).astype(BF)
        to_im = (column == row + half + n * inner).astype(BF)
        re, im = raw[0, core * blocks + n], raw[1, core * blocks + n]
        top = slice(n * inner, (n + 1) * inner)
        low = slice(half + n * inner, half + (n + 1) * inner)
        wide[top, :] = (dot(re, to_re) + dot(im, to_im)).astype(BF)
        wide[low, :] = (dot(re, to_im) - dot(im, to_re)).astype(BF)


def mix_kernel(chips, build, groups, place, *refs):
    parts, refs = refs[:chips][::-1], refs[chips:]
    lat_in, w_one, b_one, w_two, b_two, lat_out = refs[:6]
    outs = refs[6:-2]
    gathered, spread = refs[-2:]
    if build:
        wide_one, wide_two, *outs = outs
        widen(w_one, place[0] % 2, wide_one)
        widen(w_two, place[0] % 2, wide_two)
        w_one, w_two = wide_one, wide_two
    rows, count, span, half = parts[0].shape[1:]
    block = rows * span
    size = lat_in.shape[0]
    me = place[0]
    for m in range(chips):
        for e in range(2):
            first = (me ^ (2 * m + e)) * block
            for r in range(rows):
                where = pl.ds(pl.multiple_of(first + r * span, 8), span)
                for s in range(count):
                    piece = parts[m][e, r, s].astype(gathered.dtype)
                    gathered[where, s * half : (s + 1) * half] = piece
    half_bias = lambda b: jnp.concatenate(
        [b[q : q + 1, pl.ds(pl.multiple_of(me % 2 * half, 128), half)] for q in range(2)], axis=1
    )
    cut = lambda a, s: a[:, s * half : (s + 1) * half]
    modes = dot(lat_in[...], gathered[...].astype(BF)).astype(BF)
    modes = jnp.concatenate(
        [
            jnp.concatenate([cut(modes[: size // 2], s), cut(modes[size // 2 :], s)], axis=1)
            for s in range(count)
        ],
        axis=0,
    )
    first = jnp.maximum(dot(modes, w_one[...]) + half_bias(b_one), 0.0).astype(BF)
    second = dot(first, w_two[...]) + half_bias(b_two)
    second = (second - jnp.clip(second, -0.01, 0.01)).astype(BF)
    own = lambda s: second[s * size // 2 : (s + 1) * size // 2]
    second = jnp.concatenate(
        [jnp.concatenate([own(s)[:, :half], own(s)[:, half:]], axis=0) for s in range(count)],
        axis=1,
    )
    spread[...] = dot(lat_out[...], second).astype(spread.dtype)
    start = 0
    for g, rows_here in enumerate(groups):
        other, *mine = outs[g * (chips + 1) : (g + 1) * (chips + 1)]
        for m in range(chips):
            for e in range(2):
                first = (me ^ (2 * m + e)) * block
                for q in range(rows_here):
                    where = pl.ds(pl.multiple_of(first + (start + q) * span, 8), span)
                    for s in range(count):
                        piece = spread[where, s * half : (s + 1) * half].astype(BF)
                        if e == 0:
                            mine[m][q, s] = piece
                        else:
                            other[m, q, s] = piece
        start += rows_here


def mix_part(place, parts, lat_in, w_one, b_one, w_two, b_two, lat_out, groups):
    chips = len(parts)
    rows, count, span, half = parts[0].shape[1:]
    size = lat_in.shape[0]
    kind = BF if span % 16 == 0 else F32
    build = w_one.ndim == 4
    shapes = [(2 * half, 2 * half)] * 2 if build else []
    for rows_here in groups:
        piece = (rows_here, count, span, half)
        shapes += [(chips,) + piece] + [piece] * chips
    vmem = pl.BlockSpec(memory_space=pltpu.VMEM)
    operands = [*parts[::-1], lat_in, w_one, b_one, w_two, b_two, lat_out]
    out = pl.pallas_call(
        functools.partial(mix_kernel, chips, build, groups),
        in_specs=[pl.BlockSpec(memory_space=pltpu.SMEM)] + [vmem] * len(operands),
        out_specs=[vmem] * len(shapes),
        scratch_shapes=[
            pltpu.VMEM((size, count * half), kind),
            pltpu.VMEM((size, count * half), kind),
        ],
        out_shape=[jax.ShapeDtypeStruct(s, BF) for s in shapes],
        compiler_params=pltpu.CompilerParams(vmem_limit_bytes=32 * 2**20),
        cost_estimate=SMALL,
        name="mix_modes",
    )(place, *operands)
    wide, out = (out[:2], out[2:]) if build else ((w_one, w_two), out)
    return wide, [out[g * (chips + 1) : (g + 1) * (chips + 1)] for g in range(len(groups))]


def gelu(values):
    scale = math.sqrt(2.0 / math.pi)
    inner = values * (scale + (scale * 0.044715) * (values * values))
    half = 0.5 * values
    return half + half * jnp.tanh(inner)


def final_kernel(start, chips, place, *refs):
    parts, refs = refs[:chips][::-1], refs[chips:]
    base, table, gain2, shift2, fc1, bias1, fc2, bias2 = refs[:8]
    out_hbm, out, spec, mixed, act, total, sem = refs[-7:]
    count, width, samples, chans = out.shape
    tokens = width * samples
    span, half = parts[0].shape[-2:]
    chip = place[0] // 2
    core = place[0] % 2
    for q in range(count):
        for m, part in enumerate(parts):
            for e in range(2):
                lanes = pl.ds(pl.multiple_of((core ^ e) * half, 128), half)
                for s in range(samples):
                    first = pl.multiple_of(s * len(parts) * span + (chip ^ m) * span, 8)
                    spec[q, pl.ds(first, span), lanes] = part[e, q, s].astype(spec.dtype)
        state = dot(table[...], spec[q].astype(BF)) + base[start + q]
        mixed[q * tokens : (q + 1) * tokens, :] = state + bias2[...][None, :]
        normed = normalize(state, gain2[...], shift2[...]).astype(BF)
        act[q * tokens : (q + 1) * tokens, :] = normed
    hidden = fc1.shape[1]
    step = hidden // 4
    for f in range(4):
        cut = slice(f * step, (f + 1) * step)
        inner = gelu(dot(act[...], fc1[:, cut]) + bias1[cut][None, :]).astype(BF)
        piece = dot(inner, fc2[cut, :])
        if f == 0:
            total[...] = piece
        elif f < 3:
            total[...] += piece
    result = mixed[...] + (total[...] + piece)
    out[...] = result.astype(BF).reshape(out.shape)
    store = pltpu.make_async_copy(out, out_hbm.at[start : start + count], sem)
    store.start()
    store.wait()


def final_part(place, parts, base, table, vectors, mlp, start, shape, so_far):
    count = parts[0].shape[1]
    rows, width, samples, chans = shape
    kind = BF if parts[0].shape[-2] % 16 == 0 else F32
    tokens = width * samples
    vmem = pl.BlockSpec(memory_space=pltpu.VMEM)
    hbm = pl.BlockSpec(memory_space=pltpu.HBM)
    operands = [place, *parts[::-1], base, table, *vectors, *mlp]
    in_specs = [pl.BlockSpec(memory_space=pltpu.SMEM)] + [vmem] * (len(operands) - 1)
    aliases = {}
    if so_far is not None:
        aliases = {len(operands): 0}
        in_specs.append(hbm)
        operands.append(so_far)
    return pl.pallas_call(
        functools.partial(final_kernel, start, len(parts)),
        in_specs=in_specs,
        out_specs=hbm,
        scratch_shapes=[
            pltpu.VMEM((count, width, samples, chans), BF),
            pltpu.VMEM((count, samples * 2 * KW, chans), kind),
            pltpu.VMEM((count * tokens, chans), F32),
            pltpu.VMEM((count * tokens, chans), BF),
            pltpu.VMEM((count * tokens, chans), F32),
            pltpu.SemaphoreType.DMA,
        ],
        out_shape=jax.ShapeDtypeStruct(shape, BF),
        input_output_aliases=aliases,
        compiler_params=pltpu.CompilerParams(vmem_limit_bytes=36 * 2**20),
        cost_estimate=SMALL,
        name="channel_mlp",
    )(*operands)


def behind(array, earlier):
    return lax.optimization_barrier((array, earlier))[0]


def swap_cores(other, devices):
    return lax.ppermute(other, "lat", [(i, i ^ 1) for i in range(devices)])


def swap_chips(parts, devices, earlier):
    parts = list(parts)
    for m in range(len(parts) - 1, 0, -1):
        part = parts[m] if earlier is None else behind(parts[m], earlier[m])
        parts[m] = lax.ppermute(part, "lat", [(i, i ^ (2 * m)) for i in range(devices)])
    return parts


def local(devices, *args):
    (state, gain1, shift1, w_one, b_one, w_two, b_two, gain2, shift2, fc1, bias1, fc2, bias2) = args
    samples, rows, width, chans = state.shape
    chips = devices // 2
    me = lax.axis_index("lat")
    place = me.astype(jnp.int32).reshape(1)
    forward, inverse = lon_tables(width, KW, chips)
    forward = jnp.asarray(forward.astype(jnp.bfloat16))
    lat_in, lat_out = lat_tables(rows * devices, KW // chips)
    state = jnp.transpose(state, (1, 2, 0, 3))

    chunks = forward_part(place, state, gain1, shift1, forward, FIRST, chips)
    joined = []
    for pieces in chunks:
        other = swap_cores(pieces[0], devices)
        joined.append([jnp.stack([pieces[1 + m], other[m]]) for m in range(chips)])
    wide = (w_one, w_two)
    mixed = []
    for index, parts in enumerate(joined):
        if index > 0:
            light = chips // 2
            parts = [behind(p, wide[0]) for p in parts[:light]] + parts[light:]
        parts = swap_chips(parts, devices, None)
        if index == 0:
            base = residual_part(state, gain1, shift1, parts[-1])
        wide, (pieces,) = mix_part(
            place, parts, lat_in, wide[0], b_one, wide[1], b_two, lat_out, (rows,)
        )
        mixed.append((pieces[1:], swap_cores(pieces[0], devices)))

    table = jnp.asarray(over_samples(inverse.T, 0, samples, samples).T)
    returned = []
    start = 0
    for count in SECOND:
        cut = slice(start, start + count)
        joined = [
            jnp.stack(
                [
                    jnp.concatenate([own[m][cut] for own, _ in mixed], axis=1),
                    jnp.concatenate([other[m][cut] for _, other in mixed], axis=1),
                ]
            )
            for m in range(chips)
        ]
        returned.append(swap_chips(joined, devices, returned[-1] if returned else None))
        start += count

    result = None
    start = 0
    for index, parts in enumerate(returned):
        result = final_part(
            place,
            parts,
            base,
            table,
            (gain2, shift2),
            (fc1, bias1, fc2, bias2),
            start,
            state.shape,
            result,
        )
        start += SECOND[index]
    return jnp.transpose(result, (2, 0, 1, 3))


def solution(mesh):
    tokens = P("grp", "lat", None, None)
    return jax.shard_map(
        functools.partial(local, mesh.shape["lat"]),
        mesh=mesh,
        in_specs=(tokens,) + (P(),) * 12,
        out_specs=tokens,
        check_vma=False,
    )
```

```python
import functools
import math

import jax
import jax.numpy as jnp
import numpy as np
from jax import lax
from jax.experimental import pallas as pl
from jax.experimental.pallas import tpu as pltpu
from jax.sharding import PartitionSpec as P

KW = 64
BF = jnp.bfloat16
F32 = jnp.float32
SMALL = pl.CostEstimate(flops=1, bytes_accessed=1, transcendentals=0)
FIRST = (2, 2)
SECOND = (1, 1, 1)


def lon_tables(width, kept, chips):
    along = np.arange(width)
    waves = np.arange(kept)
    angle = 2.0 * math.pi / width * (along[:, None] * waves[None, :] % width)
    factor = 1.0 / math.sqrt(width)
    weight_k = np.where(waves == 0, 1.0, 2.0)
    split = (width, chips, kept // chips)
    forward = np.stack(
        [np.cos(angle).reshape(split), -np.sin(angle).reshape(split)], axis=2
    ).reshape(width, 2 * kept)
    inverse = np.stack(
        [(np.cos(angle) * weight_k).reshape(split), (-np.sin(angle) * weight_k).reshape(split)],
        axis=2,
    ).reshape(width, 2 * kept)
    return ((forward * factor).astype(np.float32).T, (inverse * factor).astype(np.float32))


def lat_tables(length, waves):
    index = np.arange(length)
    angle = 2.0 * math.pi / length * (index[:, None] * index[None, :] % length)
    cos = np.cos(angle) / math.sqrt(length)
    sin = np.sin(angle) / math.sqrt(length)
    eye = np.eye(waves)
    parts = np.array([[cos, sin], [-sin, cos]])
    size = 2 * length * waves
    forward = np.einsum("pqmh,kl->pmkhql", parts, eye).reshape(size, size)
    parts = np.array([[cos, -sin], [sin, cos]])
    inverse = np.einsum("pqhm,kl->hpkqml", parts, eye).reshape(size, size)
    to_bf = lambda t: jnp.asarray(t.astype(np.float32).astype(jnp.bfloat16))
    return to_bf(forward), to_bf(inverse)


def over_samples(table, first, count, samples):
    pick = np.eye(samples, dtype=table.dtype)[first : first + count]
    waves, width = table.shape
    wide = pick[:, None, None, :] * table[None, :, :, None]
    return jnp.asarray(wide.reshape(count * waves, width * samples).astype(jnp.bfloat16))


def normalize(values, gain, shift):
    center = jnp.mean(values, axis=-1, keepdims=True)
    away = values - center
    spread = jnp.mean(away * away, axis=-1, keepdims=True)
    return away * lax.rsqrt(spread + 1e-05) * gain[None, :] + shift[None, :]


def dot(left, right):
    return jnp.dot(left, right, preferred_element_type=F32)


def forward_kernel(place, x_hbm, gain_hbm, shift_hbm, table_hbm, *refs):
    outs = refs[:-7]
    x, flat, gain, shift, table, spec, sems = refs[-7:]
    chips, rows, _, span, half = outs[0].shape
    width, samples, chans = x_hbm.shape[1:]
    copies = [
        pltpu.make_async_copy(x_hbm.at[r], x.at[r], sems.at[r]) for r in range(rows)
    ] + [
        pltpu.make_async_copy(source, target, sems.at[rows + i])
        for i, (source, target) in enumerate(
            ((gain_hbm, gain), (shift_hbm, shift), (table_hbm, table))
        )
    ]
    for copy in copies[:1] + copies[rows:] + copies[1:rows]:
        copy.start()
    chip = place[0] // 2
    core = place[0] % 2
    for copy in copies[rows:]:
        copy.wait()
    for r in range(rows):
        copies[r].wait()
        tokens = x[r].astype(F32).reshape(width * samples, chans)
        normed = normalize(tokens, gain[...], shift[...]).astype(BF).astype(F32)
        for tile in range(flat.shape[0]):
            flat[tile] = normed[:, tile * 128 : (tile + 1) * 128]
        start = 0
        for other, *own in (outs[i : i + chips + 1] for i in range(0, len(outs), chips + 1)):
            for s in range(other.shape[2]):
                pick = pl.ds(start + s, width, stride=samples)
                values = jnp.concatenate([flat[t, pick, :] for t in range(flat.shape[0])], axis=1)
                spec[...] = dot(table[...], values.astype(BF))
                for m in range(chips):
                    where = pl.ds(pl.multiple_of((chip ^ m) * span, 8), span)
                    for e in range(2):
                        lanes = pl.ds(pl.multiple_of((core ^ e) * half, 128), half)
                        piece = spec[where, lanes].astype(BF)
                        if e == 0:
                            own[m][r, s] = piece
                        else:
                            other[m, r, s] = piece
            start += other.shape[2]


def forward_part(place, state, gain, shift, table, counts, chips):
    rows, width, samples, chans = state.shape
    waves = table.shape[0]
    outs = []
    for count in counts:
        piece = (rows, count, waves // chips, chans // 2)
        outs += [jax.ShapeDtypeStruct(s, BF) for s in [(chips,) + piece] + [piece] * chips]
    vmem = pl.BlockSpec(memory_space=pltpu.VMEM)
    hbm = pl.BlockSpec(memory_space=pltpu.HBM)
    operands = [state, gain, shift, table]
    out = pl.pallas_call(
        forward_kernel,
        in_specs=[pl.BlockSpec(memory_space=pltpu.SMEM)] + [hbm] * len(operands),
        out_specs=[vmem] * len(outs),
        scratch_shapes=[
            pltpu.VMEM(state.shape, BF),
            pltpu.VMEM((chans // 128, width * samples, 128), F32),
            pltpu.VMEM(gain.shape, F32),
            pltpu.VMEM(shift.shape, F32),
            pltpu.VMEM(table.shape, BF),
            pltpu.VMEM((waves, chans), F32),
            pltpu.SemaphoreType.DMA((rows + 3,)),
        ],
        out_shape=outs,
        compiler_params=pltpu.CompilerParams(vmem_limit_bytes=56 * 2**20),
        cost_estimate=SMALL,
        name="lon_forward",
    )(place, *operands)
    return [out[i : i + chips + 1] for i in range(0, len(out), chips + 1)]


def fill_kernel(other, *refs):
    chips = other.shape[0]
    outs, sems = refs[chips : 2 * chips], refs[-1]
    copies = [pltpu.make_async_copy(other.at[m], outs[m].at[1], sems.at[m]) for m in range(chips)]
    for copy in copies:
        copy.start()
    for copy in copies:
        copy.wait()


def fill_part(other, halves):
    anywhere = pl.BlockSpec(memory_space=pl.ANY)
    return pl.pallas_call(
        fill_kernel,
        in_specs=[anywhere] * (1 + len(halves)),
        out_specs=[anywhere] * len(halves),
        out_shape=[jax.ShapeDtypeStruct(h.shape, h.dtype) for h in halves],
        scratch_shapes=[pltpu.SemaphoreType.DMA((len(halves),))],
        input_output_aliases={1 + i: i for i in range(len(halves))},
        compiler_params=pltpu.CompilerParams(vmem_limit_bytes=16 * 2**20),
        cost_estimate=SMALL,
        name="join_cores",
    )(other, *halves)


def residual_kernel(x, gain, shift, _, out):
    for r in range(x.shape[0]):
        tokens = x[r].astype(F32).reshape(out.shape[1:])
        out[r] = tokens + normalize(tokens, gain[...], shift[...]).astype(BF).astype(F32)


def residual_part(state, gain, shift, after):
    rows, width, samples, chans = state.shape
    vmem = pl.BlockSpec(memory_space=pltpu.VMEM)
    return pl.pallas_call(
        residual_kernel,
        in_specs=[vmem] * 3 + [pl.BlockSpec(memory_space=pl.ANY)],
        out_specs=vmem,
        out_shape=jax.ShapeDtypeStruct((rows, width * samples, chans), F32),
        compiler_params=pltpu.CompilerParams(vmem_limit_bytes=16 * 2**20),
        cost_estimate=SMALL,
        name="residual",
    )(state, gain, shift, after)


def widen(raw, core, wide):
    blocks, inner = raw.shape[1] // 2, raw.shape[2]
    size = wide.shape[0]
    half = size // 2
    column = lax.broadcasted_iota(jnp.int32, (inner, size), 1)
    row = lax.broadcasted_iota(jnp.int32, (inner, size), 0)
    for n in range(blocks):
        to_re = (column == row + n * inner).astype(BF)
        to_im = (column == row + half + n * inner).astype(BF)
        re, im = raw[0, core * blocks + n], raw[1, core * blocks + n]
        top = slice(n * inner, (n + 1) * inner)
        low = slice(half + n * inner, half + (n + 1) * inner)
        wide[top, :] = (dot(re, to_re) + dot(im, to_im)).astype(BF)
        wide[low, :] = (dot(re, to_im) - dot(im, to_re)).astype(BF)


def mix_kernel(chips, build, groups, place, *refs):
    parts, refs = refs[:chips][::-1], refs[chips:]
    lat_in, w_one, b_one, w_two, b_two, lat_out = refs[:6]
    outs = refs[6:-2]
    gathered, spread = refs[-2:]
    if build:
        wide_one, wide_two, *outs = outs
        widen(w_one, place[0] % 2, wide_one)
        widen(w_two, place[0] % 2, wide_two)
        w_one, w_two = wide_one, wide_two
    rows, count, span, half = parts[0].shape[1:]
    block = rows * span
    size = lat_in.shape[0]
    me = place[0]
    for m in range(chips):
        for e in range(2):
            first = (me ^ (2 * m + e)) * block
            for r in range(rows):
                where = pl.ds(pl.multiple_of(first + r * span, 8), span)
                for s in range(count):
                    piece = parts[m][e, r, s].astype(gathered.dtype)
                    gathered[where, s * half : (s + 1) * half] = piece
    half_bias = lambda b: jnp.concatenate(
        [b[q : q + 1, pl.ds(pl.multiple_of(me % 2 * half, 128), half)] for q in range(2)], axis=1
    )
    cut = lambda a, s: a[:, s * half : (s + 1) * half]
    modes = dot(lat_in[...], gathered[...].astype(BF)).astype(BF)
    modes = jnp.concatenate(
        [
            jnp.concatenate([cut(modes[: size // 2], s), cut(modes[size // 2 :], s)], axis=1)
            for s in range(count)
        ],
        axis=0,
    )
    first = jnp.maximum(dot(modes, w_one[...]) + half_bias(b_one), 0.0).astype(BF)
    second = dot(first, w_two[...]) + half_bias(b_two)
    second = (second - jnp.clip(second, -0.01, 0.01)).astype(BF)
    own = lambda s: second[s * size // 2 : (s + 1) * size // 2]
    second = jnp.concatenate(
        [jnp.concatenate([own(s)[:, :half], own(s)[:, half:]], axis=0) for s in range(count)],
        axis=1,
    )
    spread[...] = dot(lat_out[...], second).astype(spread.dtype)
    start = 0
    for g, rows_here in enumerate(groups):
        other, *mine = outs[g * (chips + 1) : (g + 1) * (chips + 1)]
        for m in range(chips):
            for e in range(2):
                first = (me ^ (2 * m + e)) * block
                for q in range(rows_here):
                    where = pl.ds(pl.multiple_of(first + (start + q) * span, 8), span)
                    for s in range(count):
                        piece = spread[where, s * half : (s + 1) * half].astype(BF)
                        if e == 0:
                            mine[m][q, s] = piece
                        else:
                            other[m, q, s] = piece
        start += rows_here


def mix_part(place, parts, lat_in, w_one, b_one, w_two, b_two, lat_out, groups):
    chips = len(parts)
    rows, count, span, half = parts[0].shape[1:]
    size = lat_in.shape[0]
    kind = BF if span % 16 == 0 else F32
    build = w_one.ndim == 4
    shapes = [(2 * half, 2 * half)] * 2 if build else []
    for rows_here in groups:
        piece = (rows_here, count, span, half)
        shapes += [(chips,) + piece] + [piece] * chips
    vmem = pl.BlockSpec(memory_space=pltpu.VMEM)
    operands = [*parts[::-1], lat_in, w_one, b_one, w_two, b_two, lat_out]
    out = pl.pallas_call(
        functools.partial(mix_kernel, chips, build, groups),
        in_specs=[pl.BlockSpec(memory_space=pltpu.SMEM)] + [vmem] * len(operands),
        out_specs=[vmem] * len(shapes),
        scratch_shapes=[
            pltpu.VMEM((size, count * half), kind),
            pltpu.VMEM((size, count * half), kind),
        ],
        out_shape=[jax.ShapeDtypeStruct(s, BF) for s in shapes],
        compiler_params=pltpu.CompilerParams(vmem_limit_bytes=24 * 2**20),
        cost_estimate=SMALL,
        name="mix_modes",
    )(place, *operands)
    wide, out = (out[:2], out[2:]) if build else ((w_one, w_two), out)
    return wide, [out[g * (chips + 1) : (g + 1) * (chips + 1)] for g in range(len(groups))]


def gelu(values):
    scale = math.sqrt(2.0 / math.pi)
    inner = values * (scale + (scale * 0.044715) * (values * values))
    half = 0.5 * values
    return half + half * jnp.tanh(inner)


def final_kernel(start, chips, place, *refs):
    parts, refs = refs[:chips][::-1], refs[chips:]
    base, table, gain2, shift2, fc1, bias1, fc2, bias2 = refs[:8]
    out_hbm, done, out, spec, mixed, act, total, sem = refs[-8:]
    done[...] = jnp.zeros_like(done)
    count, width, samples, chans = out.shape
    tokens = width * samples
    span, half = parts[0].shape[-2:]
    chip = place[0] // 2
    core = place[0] % 2
    for q in range(count):
        for m, part in enumerate(parts):
            for e in range(2):
                lanes = pl.ds(pl.multiple_of((core ^ e) * half, 128), half)
                for s in range(samples):
                    first = pl.multiple_of(s * len(parts) * span + (chip ^ m) * span, 8)
                    spec[q, pl.ds(first, span), lanes] = part[e, q + (part.shape[1] > count) * start, s].astype(spec.dtype)
        state = dot(table[...], spec[q].astype(BF)) + base[start + q]
        mixed[q * tokens : (q + 1) * tokens, :] = state + bias2[...][None, :]
        normed = normalize(state, gain2[...], shift2[...]).astype(BF)
        act[q * tokens : (q + 1) * tokens, :] = normed
    hidden = fc1.shape[1]
    step = hidden // 4
    for f in range(4):
        cut = slice(f * step, (f + 1) * step)
        inner = gelu(dot(act[...], fc1[:, cut]) + bias1[cut][None, :]).astype(BF)
        piece = dot(inner, fc2[cut, :])
        if f == 0:
            total[...] = piece
        elif f < 3:
            total[...] += piece
    result = mixed[...] + (total[...] + piece)
    out[...] = result.astype(BF).reshape(out.shape)
    store = pltpu.make_async_copy(out, out_hbm.at[start : start + count], sem)
    store.start()
    store.wait()


def final_part(place, parts, base, table, vectors, mlp, start, count, shape, so_far):
    rows, width, samples, chans = shape
    kind = BF if parts[0].shape[-2] % 16 == 0 else F32
    tokens = width * samples
    vmem = pl.BlockSpec(memory_space=pltpu.VMEM)
    hbm = pl.BlockSpec(memory_space=pltpu.HBM)
    operands = [place, *parts[::-1], base, table, *vectors, *mlp]
    in_specs = [pl.BlockSpec(memory_space=pltpu.SMEM)] + [vmem] * (len(operands) - 1)
    aliases = {}
    if so_far is not None:
        aliases = {len(operands): 0}
        in_specs.append(hbm)
        operands.append(so_far)
    return pl.pallas_call(
        functools.partial(final_kernel, start, len(parts)),
        in_specs=in_specs,
        out_specs=[hbm, vmem],
        scratch_shapes=[
            pltpu.VMEM((count, width, samples, chans), BF),
            pltpu.VMEM((count, samples * 2 * KW, chans), kind),
            pltpu.VMEM((count * tokens, chans), F32),
            pltpu.VMEM((count * tokens, chans), BF),
            pltpu.VMEM((count * tokens, chans), F32),
            pltpu.SemaphoreType.DMA,
        ],
        out_shape=[jax.ShapeDtypeStruct(shape, BF), jax.ShapeDtypeStruct((8, 128), F32)],
        input_output_aliases=aliases,
        compiler_params=pltpu.CompilerParams(vmem_limit_bytes=20 * 2**20),
        cost_estimate=SMALL,
        name="channel_mlp",
    )(*operands)


def behind(array, earlier):
    return lax.optimization_barrier((array, earlier))[0]


def swap_cores(other, devices):
    return lax.ppermute(other, "lat", [(i, i ^ 1) for i in range(devices)])


def swap_chips(parts, first, devices):
    parts = list(parts)
    for n in range(len(parts) - 1, -1, -1):
        m = first + n
        if m > 0:
            pairs = [(i, i ^ (2 * m)) for i in range(devices)]
            parts[n] = lax.ppermute(parts[n], "lat", pairs)
    return parts


def local(devices, *args):
    (state, gain1, shift1, w_one, b_one, w_two, b_two, gain2, shift2, fc1, bias1, fc2, bias2) = args
    samples, rows, width, chans = state.shape
    chips = devices // 2
    me = lax.axis_index("lat")
    place = me.astype(jnp.int32).reshape(1)
    forward, inverse = lon_tables(width, KW, chips)
    forward = jnp.asarray(forward.astype(jnp.bfloat16))
    lat_in, lat_out = lat_tables(rows * devices, KW // chips)
    state = jnp.transpose(state, (1, 2, 0, 3))

    chunks = forward_part(place, state, gain1, shift1, forward, FIRST, chips)
    joined = []
    light = chips // 2
    for pieces in chunks:
        other = swap_cores(pieces[0], devices)
        joined.append([jnp.stack([pieces[1 + m], other[m]]) for m in range(chips)])
    wide = (w_one, w_two)
    mixed = []
    for index, parts in enumerate(joined):
        if index > 0:
            parts = [behind(p, wide[0]) for p in parts[:light]] + parts[light:]
        parts = swap_chips(parts, 0, devices)
        if index == 0:
            base = residual_part(state, gain1, shift1, parts[-1])
        wide, (pieces,) = mix_part(
            place, parts, lat_in, wide[0], b_one, wide[1], b_two, lat_out, (rows,)
        )
        mixed.append((pieces[1:], swap_cores(pieces[0], devices)))

    table = jnp.asarray(over_samples(inverse.T, 0, samples, samples).T)
    def join(m, first, count):
        cut = slice(first, first + count)
        return jnp.stack(
            [
                jnp.concatenate([own[m][cut] for own, _ in mixed], axis=1),
                jnp.concatenate([other[m][cut] for _, other in mixed], axis=1),
            ]
        )

    near = swap_chips([join(m, 0, rows) for m in range(light)], 0, devices)
    result = None
    far = None
    marks = []
    start = 0
    for index, count in enumerate(SECOND):
        pieces = [join(m, start, count) for m in range(light, chips)]
        if index < 0:
            pieces = [behind(p, f) for p, f in zip(pieces, far)]
        if index > 1:
            pieces = [behind(p, marks[index - 2]) for p in pieces]
        far = swap_chips(pieces, light, devices)
        result, done = final_part(
            place,
            near + far,
            base,
            table,
            (gain2, shift2),
            (fc1, bias1, fc2, bias2),
            start,
            count,
            state.shape,
            result,
        )
        marks.append(done)
        start += count
    return jnp.transpose(result, (2, 0, 1, 3))


def solution(mesh):
    tokens = P("grp", "lat", None, None)
    return jax.shard_map(
        functools.partial(local, mesh.shape["lat"]),
        mesh=mesh,
        in_specs=(tokens,) + (P(),) * 12,
        out_specs=tokens,
        check_vma=False,
    )
```

```python
import functools
import math

import jax
import jax.numpy as jnp
import numpy as np
from jax import lax
from jax.experimental import pallas as pl
from jax.experimental.pallas import tpu as pltpu
from jax.sharding import PartitionSpec as P

KW = 64
BF = jnp.bfloat16
F32 = jnp.float32
SMALL = pl.CostEstimate(flops=1, bytes_accessed=1, transcendentals=0)
FIRST = (2, 2)
SECOND = (1, 1, 1)


def lon_tables(width, kept, chips):
    along = np.arange(width)
    waves = np.arange(kept)
    angle = 2.0 * math.pi / width * (along[:, None] * waves[None, :] % width)
    factor = 1.0 / math.sqrt(width)
    weight_k = np.where(waves == 0, 1.0, 2.0)
    split = (width, chips, kept // chips)
    forward = np.stack(
        [np.cos(angle).reshape(split), -np.sin(angle).reshape(split)], axis=2
    ).reshape(width, 2 * kept)
    inverse = np.stack(
        [(np.cos(angle) * weight_k).reshape(split), (-np.sin(angle) * weight_k).reshape(split)],
        axis=2,
    ).reshape(width, 2 * kept)
    return ((forward * factor).astype(np.float32).T, (inverse * factor).astype(np.float32))


def lat_tables(length, waves):
    index = np.arange(length)
    angle = 2.0 * math.pi / length * (index[:, None] * index[None, :] % length)
    cos = np.cos(angle) / math.sqrt(length)
    sin = np.sin(angle) / math.sqrt(length)
    eye = np.eye(waves)
    parts = np.array([[cos, sin], [-sin, cos]])
    size = 2 * length * waves
    forward = np.einsum("pqmh,kl->pmkhql", parts, eye).reshape(size, size)
    parts = np.array([[cos, -sin], [sin, cos]])
    inverse = np.einsum("pqhm,kl->hpkqml", parts, eye).reshape(size, size)
    to_bf = lambda t: jnp.asarray(t.astype(np.float32).astype(jnp.bfloat16))
    return to_bf(forward), to_bf(inverse)


def over_samples(table, first, count, samples):
    pick = np.eye(samples, dtype=table.dtype)[first : first + count]
    waves, width = table.shape
    wide = pick[:, None, None, :] * table[None, :, :, None]
    return jnp.asarray(wide.reshape(count * waves, width * samples).astype(jnp.bfloat16))


def normalize(values, gain, shift):
    center = jnp.mean(values, axis=-1, keepdims=True)
    away = values - center
    spread = jnp.mean(away * away, axis=-1, keepdims=True)
    return away * lax.rsqrt(spread + 1e-05) * gain[None, :] + shift[None, :]


def dot(left, right):
    return jnp.dot(left, right, preferred_element_type=F32)


def forward_kernel(place, x_hbm, gain_hbm, shift_hbm, table_hbm, *refs):
    outs = refs[:-7]
    x, flat, gain, shift, table, spec, sems = refs[-7:]
    chips, rows, _, span, half = outs[0].shape
    width, samples, chans = x_hbm.shape[1:]
    copies = [
        pltpu.make_async_copy(x_hbm.at[r], x.at[r], sems.at[r]) for r in range(rows)
    ] + [
        pltpu.make_async_copy(source, target, sems.at[rows + i])
        for i, (source, target) in enumerate(
            ((gain_hbm, gain), (shift_hbm, shift), (table_hbm, table))
        )
    ]
    for copy in copies[:1] + copies[rows:] + copies[1:rows]:
        copy.start()
    chip = place[0] // 2
    core = place[0] % 2
    for copy in copies[rows:]:
        copy.wait()
    for r in range(rows):
        copies[r].wait()
        tokens = x[r].astype(F32).reshape(width * samples, chans)
        normed = normalize(tokens, gain[...], shift[...]).astype(BF).astype(F32)
        for tile in range(flat.shape[0]):
            flat[tile, : width * samples] = normed[:, tile * 128 : (tile + 1) * 128]
        start = 0
        for other, *own in (outs[i : i + chips + 1] for i in range(0, len(outs), chips + 1)):
            for s in range(other.shape[2]):
                pick = pl.ds(start + s, width, stride=samples)
                values = jnp.concatenate([flat[t, pick, :] for t in range(flat.shape[0])], axis=1)
                spec[...] = dot(table[...], values.astype(BF))
                for m in range(chips):
                    where = pl.ds(pl.multiple_of((chip ^ m) * span, 8), span)
                    for e in range(2):
                        lanes = pl.ds(pl.multiple_of((core ^ e) * half, 128), half)
                        piece = spec[where, lanes].astype(BF)
                        if e == 0:
                            own[m][r, s] = piece
                        else:
                            other[m, r, s] = piece
            start += other.shape[2]


def forward_part(place, state, gain, shift, table, counts, chips):
    rows, width, samples, chans = state.shape
    waves = table.shape[0]
    outs = []
    for count in counts:
        piece = (rows, count, waves // chips, chans // 2)
        outs += [jax.ShapeDtypeStruct(s, BF) for s in [(chips,) + piece] + [piece] * chips]
    vmem = pl.BlockSpec(memory_space=pltpu.VMEM)
    hbm = pl.BlockSpec(memory_space=pltpu.HBM)
    operands = [state, gain, shift, table]
    out = pl.pallas_call(
        forward_kernel,
        in_specs=[pl.BlockSpec(memory_space=pltpu.SMEM)] + [hbm] * len(operands),
        out_specs=[vmem] * len(outs),
        scratch_shapes=[
            pltpu.VMEM(state.shape, BF),
            pltpu.VMEM((chans // 128, (width + 7) // 8 * 8 * samples, 128), F32),
            pltpu.VMEM(gain.shape, F32),
            pltpu.VMEM(shift.shape, F32),
            pltpu.VMEM(table.shape, BF),
            pltpu.VMEM((waves, chans), F32),
            pltpu.SemaphoreType.DMA((rows + 3,)),
        ],
        out_shape=outs,
        compiler_params=pltpu.CompilerParams(vmem_limit_bytes=56 * 2**20),
        cost_estimate=SMALL,
        name="lon_forward",
    )(place, *operands)
    return [out[i : i + chips + 1] for i in range(0, len(out), chips + 1)]


def fill_kernel(other, *refs):
    chips = other.shape[0]
    outs, sems = refs[chips : 2 * chips], refs[-1]
    copies = [pltpu.make_async_copy(other.at[m], outs[m].at[1], sems.at[m]) for m in range(chips)]
    for copy in copies:
        copy.start()
    for copy in copies:
        copy.wait()


def fill_part(other, halves):
    anywhere = pl.BlockSpec(memory_space=pl.ANY)
    return pl.pallas_call(
        fill_kernel,
        in_specs=[anywhere] * (1 + len(halves)),
        out_specs=[anywhere] * len(halves),
        out_shape=[jax.ShapeDtypeStruct(h.shape, h.dtype) for h in halves],
        scratch_shapes=[pltpu.SemaphoreType.DMA((len(halves),))],
        input_output_aliases={1 + i: i for i in range(len(halves))},
        compiler_params=pltpu.CompilerParams(vmem_limit_bytes=16 * 2**20),
        cost_estimate=SMALL,
        name="join_cores",
    )(other, *halves)


def residual_kernel(x, gain, shift, _, out):
    for r in range(x.shape[0]):
        tokens = x[r].astype(F32).reshape(out.shape[1:])
        out[r] = tokens + normalize(tokens, gain[...], shift[...]).astype(BF).astype(F32)


def residual_part(state, gain, shift, after):
    rows, width, samples, chans = state.shape
    vmem = pl.BlockSpec(memory_space=pltpu.VMEM)
    return pl.pallas_call(
        residual_kernel,
        in_specs=[vmem] * 3 + [pl.BlockSpec(memory_space=pl.ANY)],
        out_specs=vmem,
        out_shape=jax.ShapeDtypeStruct((rows, width * samples, chans), F32),
        compiler_params=pltpu.CompilerParams(vmem_limit_bytes=16 * 2**20),
        cost_estimate=SMALL,
        name="residual",
    )(state, gain, shift, after)


def widen(raw, core, wide):
    blocks, inner = raw.shape[1] // 2, raw.shape[2]
    size = wide.shape[0]
    half = size // 2
    column = lax.broadcasted_iota(jnp.int32, (inner, size), 1)
    row = lax.broadcasted_iota(jnp.int32, (inner, size), 0)
    for n in range(blocks):
        to_re = (column == row + n * inner).astype(BF)
        to_im = (column == row + half + n * inner).astype(BF)
        re, im = raw[0, core * blocks + n], raw[1, core * blocks + n]
        top = slice(n * inner, (n + 1) * inner)
        low = slice(half + n * inner, half + (n + 1) * inner)
        wide[top, :] = (dot(re, to_re) + dot(im, to_im)).astype(BF)
        wide[low, :] = (dot(re, to_im) - dot(im, to_re)).astype(BF)


def mix_kernel(chips, build, groups, place, *refs):
    parts, refs = refs[:chips][::-1], refs[chips:]
    lat_in, w_one, b_one, w_two, b_two, lat_out = refs[:6]
    outs = refs[6:-2]
    gathered, spread = refs[-2:]
    if build:
        wide_one, wide_two, *outs = outs
        widen(w_one, place[0] % 2, wide_one)
        widen(w_two, place[0] % 2, wide_two)
        w_one, w_two = wide_one, wide_two
    rows, count, span, half = parts[0].shape[1:]
    block = rows * span
    size = lat_in.shape[0]
    me = place[0]
    for m in range(chips):
        for e in range(2):
            first = (me ^ (2 * m + e)) * block
            for r in range(rows):
                where = pl.ds(pl.multiple_of(first + r * span, 8), span)
                for s in range(count):
                    piece = parts[m][e, r, s].astype(gathered.dtype)
                    gathered[where, s * half : (s + 1) * half] = piece
    half_bias = lambda b: jnp.concatenate(
        [b[q : q + 1, pl.ds(pl.multiple_of(me % 2 * half, 128), half)] for q in range(2)], axis=1
    )
    cut = lambda a, s: a[:, s * half : (s + 1) * half]
    modes = dot(lat_in[...], gathered[...].astype(BF)).astype(BF)
    modes = jnp.concatenate(
        [
            jnp.concatenate([cut(modes[: size // 2], s), cut(modes[size // 2 :], s)], axis=1)
            for s in range(count)
        ],
        axis=0,
    )
    first = jnp.maximum(dot(modes, w_one[...]) + half_bias(b_one), 0.0).astype(BF)
    second = dot(first, w_two[...]) + half_bias(b_two)
    second = (second - jnp.clip(second, -0.01, 0.01)).astype(BF)
    own = lambda s: second[s * size // 2 : (s + 1) * size // 2]
    second = jnp.concatenate(
        [jnp.concatenate([own(s)[:, :half], own(s)[:, half:]], axis=0) for s in range(count)],
        axis=1,
    )
    spread[...] = dot(lat_out[...], second).astype(spread.dtype)
    start = 0
    for g, rows_here in enumerate(groups):
        other, *mine = outs[g * (chips + 1) : (g + 1) * (chips + 1)]
        for m in range(chips):
            for e in range(2):
                first = (me ^ (2 * m + e)) * block
                for q in range(rows_here):
                    where = pl.ds(pl.multiple_of(first + (start + q) * span, 8), span)
                    for s in range(count):
                        piece = spread[where, s * half : (s + 1) * half].astype(BF)
                        if e == 0:
                            mine[m][q, s] = piece
                        else:
                            other[m, q, s] = piece
        start += rows_here


def mix_part(place, parts, lat_in, w_one, b_one, w_two, b_two, lat_out, groups):
    chips = len(parts)
    rows, count, span, half = parts[0].shape[1:]
    size = lat_in.shape[0]
    kind = BF if span % 16 == 0 else F32
    build = w_one.ndim == 4
    shapes = [(2 * half, 2 * half)] * 2 if build else []
    for rows_here in groups:
        piece = (rows_here, count, span, half)
        shapes += [(chips,) + piece] + [piece] * chips
    vmem = pl.BlockSpec(memory_space=pltpu.VMEM)
    operands = [*parts[::-1], lat_in, w_one, b_one, w_two, b_two, lat_out]
    out = pl.pallas_call(
        functools.partial(mix_kernel, chips, build, groups),
        in_specs=[pl.BlockSpec(memory_space=pltpu.SMEM)] + [vmem] * len(operands),
        out_specs=[vmem] * len(shapes),
        scratch_shapes=[
            pltpu.VMEM((size, count * half), kind),
            pltpu.VMEM((size, count * half), kind),
        ],
        out_shape=[jax.ShapeDtypeStruct(s, BF) for s in shapes],
        compiler_params=pltpu.CompilerParams(vmem_limit_bytes=24 * 2**20),
        cost_estimate=SMALL,
        name="mix_modes",
    )(place, *operands)
    wide, out = (out[:2], out[2:]) if build else ((w_one, w_two), out)
    return wide, [out[g * (chips + 1) : (g + 1) * (chips + 1)] for g in range(len(groups))]


def gelu(values):
    scale = math.sqrt(2.0 / math.pi)
    inner = values * (scale + (scale * 0.044715) * (values * values))
    half = 0.5 * values
    return half + half * jnp.tanh(inner)


def final_kernel(start, chips, place, *refs):
    parts, refs = refs[:chips][::-1], refs[chips:]
    base, table, gain2, shift2, fc1, bias1, fc2, bias2 = refs[:8]
    out_hbm, done, out, spec, mixed, act, total, sem = refs[-8:]
    done[...] = jnp.zeros_like(done)
    count, width, samples, chans = out.shape
    tokens = width * samples
    span, half = parts[0].shape[-2:]
    chip = place[0] // 2
    core = place[0] % 2
    for q in range(count):
        for m, part in enumerate(parts):
            for e in range(2):
                lanes = pl.ds(pl.multiple_of((core ^ e) * half, 128), half)
                for s in range(samples):
                    first = pl.multiple_of(s * len(parts) * span + (chip ^ m) * span, 8)
                    spec[q, pl.ds(first, span), lanes] = part[e, q + (part.shape[1] > count) * start, s].astype(spec.dtype)
        state = dot(table[...], spec[q].astype(BF)) + base[start + q]
        mixed[q * tokens : (q + 1) * tokens, :] = state + bias2[...][None, :]
        normed = normalize(state, gain2[...], shift2[...]).astype(BF)
        act[q * tokens : (q + 1) * tokens, :] = normed
    hidden = fc1.shape[1]
    step = hidden // 4
    for f in range(4):
        cut = slice(f * step, (f + 1) * step)
        inner = gelu(dot(act[...], fc1[:, cut]) + bias1[cut][None, :]).astype(BF)
        piece = dot(inner, fc2[cut, :])
        if f == 0:
            total[...] = piece
        elif f < 3:
            total[...] += piece
    result = mixed[...] + (total[...] + piece)
    out[...] = result.astype(BF).reshape(out.shape)
    store = pltpu.make_async_copy(out, out_hbm.at[start : start + count], sem)
    store.start()
    store.wait()


def final_part(place, parts, base, table, vectors, mlp, start, count, shape, so_far):
    rows, width, samples, chans = shape
    kind = BF if parts[0].shape[-2] % 16 == 0 else F32
    tokens = width * samples
    vmem = pl.BlockSpec(memory_space=pltpu.VMEM)
    hbm = pl.BlockSpec(memory_space=pltpu.HBM)
    operands = [place, *parts[::-1], base, table, *vectors, *mlp]
    in_specs = [pl.BlockSpec(memory_space=pltpu.SMEM)] + [vmem] * (len(operands) - 1)
    aliases = {}
    if so_far is not None:
        aliases = {len(operands): 0}
        in_specs.append(hbm)
        operands.append(so_far)
    return pl.pallas_call(
        functools.partial(final_kernel, start, len(parts)),
        in_specs=in_specs,
        out_specs=[hbm, vmem],
        scratch_shapes=[
            pltpu.VMEM((count, width, samples, chans), BF),
            pltpu.VMEM((count, samples * 2 * KW, chans), kind),
            pltpu.VMEM((count * tokens, chans), F32),
            pltpu.VMEM((count * tokens, chans), BF),
            pltpu.VMEM((count * tokens, chans), F32),
            pltpu.SemaphoreType.DMA,
        ],
        out_shape=[jax.ShapeDtypeStruct(shape, BF), jax.ShapeDtypeStruct((8, 128), F32)],
        input_output_aliases=aliases,
        compiler_params=pltpu.CompilerParams(vmem_limit_bytes=20 * 2**20),
        cost_estimate=SMALL,
        name="channel_mlp",
    )(*operands)


def behind(array, earlier):
    return lax.optimization_barrier((array, earlier))[0]


def swap_cores(other, devices):
    return lax.ppermute(other, "lat", [(i, i ^ 1) for i in range(devices)])


def swap_chips(parts, first, devices):
    parts = list(parts)
    for n in range(len(parts) - 1, -1, -1):
        m = first + n
        if m > 0:
            pairs = [(i, i ^ (2 * m)) for i in range(devices)]
            parts[n] = lax.ppermute(parts[n], "lat", pairs)
    return parts


def local(devices, *args):
    (state, gain1, shift1, w_one, b_one, w_two, b_two, gain2, shift2, fc1, bias1, fc2, bias2) = args
    samples, rows, width, chans = state.shape
    chips = devices // 2
    me = lax.axis_index("lat")
    place = me.astype(jnp.int32).reshape(1)
    forward, inverse = lon_tables(width, KW, chips)
    forward = jnp.asarray(forward.astype(jnp.bfloat16))
    lat_in, lat_out = lat_tables(rows * devices, KW // chips)
    state = jnp.transpose(state, (1, 2, 0, 3))

    chunks = forward_part(place, state, gain1, shift1, forward, FIRST, chips)
    joined = []
    light = chips // 2
    for pieces in chunks:
        other = swap_cores(pieces[0], devices)
        joined.append([jnp.stack([pieces[1 + m], other[m]]) for m in range(chips)])
    wide = (w_one, w_two)
    mixed = []
    for index, parts in enumerate(joined):
        if index > 0:
            parts = [behind(p, wide[0]) for p in parts[:light]] + parts[light:]
        parts = swap_chips(parts, 0, devices)
        if index == 0:
            base = residual_part(state, gain1, shift1, parts[-1])
        wide, (pieces,) = mix_part(
            place, parts, lat_in, wide[0], b_one, wide[1], b_two, lat_out, (rows,)
        )
        mixed.append((pieces[1:], swap_cores(pieces[0], devices)))

    table = jnp.asarray(over_samples(inverse.T, 0, samples, samples).T)
    def join(m, first, count):
        cut = slice(first, first + count)
        return jnp.stack(
            [
                jnp.concatenate([own[m][cut] for own, _ in mixed], axis=1),
                jnp.concatenate([other[m][cut] for _, other in mixed], axis=1),
            ]
        )

    near = swap_chips([join(m, 0, rows) for m in range(light)], 0, devices)
    result = None
    far = None
    marks = []
    start = 0
    for index, count in enumerate(SECOND):
        pieces = [join(m, start, count) for m in range(light, chips)]
        if index < 0:
            pieces = [behind(p, f) for p, f in zip(pieces, far)]
        if index > 1:
            pieces = [behind(p, marks[index - 2]) for p in pieces]
        far = swap_chips(pieces, light, devices)
        result, done = final_part(
            place,
            near + far,
            base,
            table,
            (gain2, shift2),
            (fc1, bias1, fc2, bias2),
            start,
            count,
            state.shape,
            result,
        )
        marks.append(done)
        start += count
    return jnp.transpose(result, (2, 0, 1, 3))


def solution(mesh):
    tokens = P("grp", "lat", None, None)
    return jax.shard_map(
        functools.partial(local, mesh.shape["lat"]),
        mesh=mesh,
        in_specs=(tokens,) + (P(),) * 12,
        out_specs=tokens,
        check_vma=False,
    )
```
